32 devices in a mesh: members: 2 (over y), wave: 4 (over z), lev: 2 (over x), fld: 2 (over core).
Axes of the slice: x: 2, y: 2, z: 4, core: 2. Of those that a mesh axis runs over, the one named last changes fastest.
Arguments:
- spec_main: bfloat16 [4, 96, 384, 1536], P(('members', 'fld'), 'lev', 'wave'), parts along dimension 0, may hold values from -6 to 6
- spec_diag: bfloat16 [4, 96, 768], P(('members', 'fld'), 'lev', 'wave'), parts along dimension 0, may hold values from -6 to 6
- pair_slots: int32 [384], P('wave'), may hold values from 0 to 383, each once
- correlation: bfloat16 [384, 2, 2, 96, 96], P(('wave', 'lev'), None, 'fld'), may hold values from -0.625 to 0.625
- balance: bfloat16 [384, 2, 96, 96], P(('wave', 'lev')), may hold values from -0.625 to 0.625
- legendre: bfloat16 [384, 32, 768], P('wave'), may hold values from -0.01171875 to 0.01171875
- legendre_diag: bfloat16 [384, 32], P('wave'), may hold values from -0.21875 to 0.21875
Outputs:
- grid_fields: float32 [4, 96, 32, 128], P(('members', 'fld'), 'lev', 'wave'), parts along dimension 0
The draws below stay inside these ranges and needn't reach their ends.
There are 2 independent parts, one for each index of `members`. The reference program is written for one: setup_inputs(seed, part) draws one part's arguments, and reference() takes and returns one part's arrays. A program takes and returns all parts, laid end to end along the dimension named above; an argument that names none is the same for every part. Nothing has to cross between parts.
Inputs may be any that keep to these rules, and one draw needn't show every extreme that they name: pair_slots holds every pair once: slot r carries the orders pair_slots[r] and 767 - pair_slots[r].
All inputs are finite; a program needn't handle non-finite values.
Results may differ from the reference program's by a relative error of at most 0.0034.
Values may be sent and summed in bfloat16 or wider, within the bound.
A program may use at most 256 MiB of HBM per device.

```python
import math
import jax
import jax.numpy as jnp
from jax import lax

NWAVE = 768
NPAIRS = 384
LEVELS = 96
FLD = 2
NLAT = 32
NLON = 128


def spiked(drawn, rng, source, target, parts, factor):
    owner, partner = [(jnp.arange(drawn.shape[dim]) // (drawn.shape[dim] // parts)).reshape([-1 if axis == dim else 1 for axis in range(drawn.ndim)]) for dim in (source, target)]
    chosen = jax.random.permutation(rng, parts)[partner]
    strong = (owner == chosen) | (owner == (partner + parts // 2) % parts)
    return jnp.where(strong, factor * drawn, drawn)


def block_levels(key, dims, cuts, low, largest):
    def one(dim, shards_of):
        heights = jax.random.uniform(jax.random.fold_in(jax.random.fold_in(key, 6), dim), (shards_of,), jnp.float32, low / len(cuts), largest / len(cuts))
        return jnp.repeat(jnp.exp(heights), dims[dim] // shards_of).reshape((-1,) + (1,) * (len(dims) - dim - 1))

    gain = one(*cuts[0])
    for cut in cuts[1:]:
        gain = gain * one(*cut)
    return gain


def gaussian(rng, dims, width, limit, cuts=(), kind=jnp.bfloat16):
    factor_of = block_levels(rng, dims, cuts, -0.22, 0.18) if cuts else 1.0
    result = jax.random.normal(rng, dims, jnp.float32) * width * factor_of
    return jnp.minimum(jnp.maximum(result, -limit), limit).astype(kind)


def heavy_noise(own_key, dims, deviation, limit, pieces, heavy, kind=jnp.bfloat16):
    drawn = deviation * jax.random.normal(own_key, dims, jnp.float32)
    if pieces:
        drawn = drawn * block_levels(own_key, dims, pieces, -0.22, 0.18)
    return jnp.clip(spiked(drawn, jax.random.fold_in(own_key, 3), *heavy), -limit, limit).astype(kind)


def setup_inputs(seed: int = 0, part: int = 0) -> dict:
    splits = jax.random.split(jax.random.key(seed), 8)
    own_keys = jax.random.split(jax.random.fold_in(splits[7], part), 8)
    return {
        "spec_main": gaussian(own_keys[0], (FLD, LEVELS, NPAIRS, 4 * NPAIRS), 1.0, 6.0, ((0, 2), (1, 2), (2, 4))),
        "spec_diag": gaussian(own_keys[1], (FLD, LEVELS, 2 * NPAIRS), 1.0, 6.0, ((0, 2), (1, 2), (2, 4))),
        "pair_slots": jax.random.permutation(splits[2], NPAIRS).astype(jnp.int32),
        "correlation": gaussian(splits[3], (NPAIRS, 2, FLD, LEVELS, LEVELS), LEVELS ** -0.5, 0.625, ((0, 8), (2, 2))),
        "balance": gaussian(splits[4], (NPAIRS, 2, LEVELS, LEVELS), LEVELS ** -0.5, 0.625, ((0, 8),)),
        "legendre": heavy_noise(splits[5], (NPAIRS, NLAT, 2 * NPAIRS), (NWAVE * NWAVE) ** -0.5, 0.01171875, ((0, 4),), (0, 1, 4, 2.0)),
        "legendre_diag": gaussian(splits[6], (NPAIRS, NLAT), NWAVE ** -0.5, 0.21875, ((0, 4),)),
    }


def order_table(orders, length):
    columns = jnp.arange(length, dtype=jnp.int32)
    phases = (orders[..., None] * columns) % (2 * NWAVE)
    angles = phases.astype(jnp.float32) * (math.pi / NWAVE)
    weight = jnp.where(orders == 0, 1.0, 2.0).astype(jnp.float32)[..., None]
    return jnp.stack([weight * jnp.cos(angles), -weight * jnp.sin(angles)], axis=-2)


def pair_block(inputs):
    block_values, diag_vector, matrices, couplings, lower_mask = inputs
    values = block_values.astype(jnp.float32)
    upper_part = jnp.einsum("fkl,flrsc->fkrsc", matrices[1].astype(jnp.float32), values)
    lower_part = jnp.einsum("fkl,flrc->fkrc", matrices[0].astype(jnp.float32), values[:, :, :, 1])
    second = (jnp.arange(2) == 1)[None, None, None, :, None]
    picked = second & lower_mask[None, None, :, None, None]
    correlated = jnp.where(picked, lower_part[:, :, :, None, :], upper_part)
    sent_field = lax.optimization_barrier(correlated[0].astype(jnp.bfloat16))
    sent_float = sent_field.astype(jnp.float32)
    coupled_upper = jnp.einsum("kl,lrsc->krsc", couplings[1].astype(jnp.float32), sent_float)
    coupled_lower = jnp.einsum("kl,lrc->krc", couplings[0].astype(jnp.float32), sent_float[:, :, 1])
    coupled = jnp.where(picked[0], coupled_lower[:, :, None, :], coupled_upper)
    balanced = jnp.stack([sent_field, (correlated[1] + coupled).astype(jnp.bfloat16)])
    diag_corr = jnp.einsum("fkl,flc->fkc", matrices[1].astype(jnp.float32), diag_vector.astype(jnp.float32))
    diag_sent = diag_corr[0].astype(jnp.bfloat16)
    diag_coupled = jnp.dot(couplings[1], diag_sent, preferred_element_type=jnp.float32)
    diag_balanced = jnp.stack([diag_sent, (diag_corr[1] + diag_coupled).astype(jnp.bfloat16)])
    return balanced, diag_balanced


def reference(spec_main, spec_diag, pair_slots, correlation, balance, legendre, legendre_diag):
    slot_index = jnp.arange(NPAIRS, dtype=jnp.int32)
    slot_of_pair = jnp.zeros((NPAIRS,), jnp.int32).at[pair_slots].set(slot_index)
    entries = jnp.moveaxis(spec_main.reshape(FLD, LEVELS, NPAIRS, NPAIRS, 2, 2), 3, 0)
    diag_all = spec_diag.reshape(FLD, LEVELS, NPAIRS, 2)
    diag_by_pair = jnp.moveaxis(diag_all[:, :, slot_of_pair], 2, 0)
    lower_all = slot_index[:, None] >= pair_slots[None, :]
    balanced, diag_balanced = lax.map(pair_block, (entries, diag_by_pair, correlation, balance, lower_all))
    tables = legendre.reshape(NPAIRS, NLAT, NPAIRS, 2)
    diag_slot = diag_balanced[pair_slots]

    def slot_block(inputs):
        slot_number, table_rows, sector_row, diag_vector = inputs
        values = lax.dynamic_index_in_dim(balanced, slot_number, 3, keepdims=False).astype(jnp.float32)
        own_lower = slot_index >= pair_slots[slot_number]
        table_float = table_rows.astype(jnp.float32)
        first_part = jnp.einsum("jb,bfkc->fkjc", table_float[:, :, 0], values[:, :, :, 0])
        first_part = first_part + jnp.einsum("jb,bfkc->fkjc", table_float[:, :, 1] * own_lower, values[:, :, :, 1])
        second_part = jnp.einsum("jb,bfkc->fkjc", table_float[:, :, 1] * (~own_lower), values[:, :, :, 1])
        second_part = second_part + sector_row.astype(jnp.float32)[None, None, :, None] * diag_vector.astype(jnp.float32)[:, :, None, :]
        return jnp.stack([first_part, second_part], axis=3)

    coeffs = lax.map(slot_block, (slot_index, tables, legendre_diag, diag_slot))
    orders = jnp.stack([pair_slots, NWAVE - 1 - pair_slots], axis=1)
    fourier_table = order_table(orders, NLON)
    return jnp.einsum("rfkjic,ricl->fkjl", coeffs, fourier_table, precision=lax.Precision.HIGHEST)
```

```python
import functools
import math

import jax
import jax.numpy as jnp
from jax import lax
from jax.experimental import pallas as pl
from jax.experimental.pallas import tpu as pltpu
from jax.sharding import PartitionSpec as P

NWAVE = 768
NLON = 128
STEP = 64
LANES = 128


def order_table(orders, length):
    columns = jnp.arange(length, dtype=jnp.int32)
    phases = orders[..., None] * columns % (2 * NWAVE)
    angles = phases.astype(jnp.float32) * (math.pi / NWAVE)
    weight = jnp.where(orders == 0, 1.0, 2.0).astype(jnp.float32)[..., None]
    return jnp.stack([weight * jnp.cos(angles), -weight * jnp.sin(angles)], axis=-2)


def synth_kernel(group, rows, levels, lats, ids_ref, low_ref, x_ref, xd_ref, w_ref, p_ref,
                 out_ref, diag_ref, ysc, acc):
    step = pl.program_id(0)
    steps = pl.num_programs(0)
    orders = jnp.concatenate([low_ref[...], low_ref[...]], axis=0)

    def unit_group(g, carry):
        for e in range(group):
            u = g * group + e
            w = w_ref[g]
            base = e * 2 * levels
            w_low = w[:, base:base + levels]
            w_up = w[:, base + levels:base + 2 * levels]
            first = x_ref[u, 0].reshape(2 * rows, x_ref.shape[-1])
            second = x_ref[u, 1].reshape(2 * rows, x_ref.shape[-1])
            y0 = jnp.dot(first, w_up, preferred_element_type=jnp.float32)
            y1u = jnp.dot(second, w_up, preferred_element_type=jnp.float32)
            y1l = jnp.dot(second, w_low, preferred_element_type=jnp.float32)
            diag_ref[u, :, 0:levels] = jnp.dot(xd_ref[u], w_up, preferred_element_type=jnp.float32)
            b = ids_ref[step * STEP + u]
            y1 = jnp.where(orders <= b, y1l, y1u)
            for c in range(2):
                for s, y in ((0, y0), (1, y1)):
                    ysc[c, pl.ds(2 * u + s, rows, stride=2 * STEP), 0:levels] = (
                        y[c * rows:(c + 1) * rows])
        return carry

    lax.fori_loop(0, STEP // group, unit_group, 0)

    @pl.when(step == 0)
    def _():
        acc[...] = jnp.zeros_like(acc)

    def slot(r, carry):
        start = pl.multiple_of(r * 2 * STEP, 2 * STEP)
        table = p_ref[r]
        for c in range(2):
            y = ysc[c, pl.ds(start, 2 * STEP), :].astype(jnp.bfloat16)
            acc[r, c] += jnp.dot(table, y, preferred_element_type=jnp.float32)
        return carry

    lax.fori_loop(0, rows, slot, 0)

    @pl.when(step == steps - 1)
    def _():
        def spread(r, carry):
            for c in range(2):
                for i in range(2):
                    out_ref[pl.ds(r * 4 + i * 2 + c, lats, stride=4 * rows), :] = (
                        acc[r, c, i * lats:(i + 1) * lats])
            return carry

        lax.fori_loop(0, rows, spread, 0)


def synthesize(ids, low, x, xd, w, tables, levels):
    units, _, _, rows, part = x.shape
    lats = tables.shape[1] // 2
    group = w.shape[-1] // (2 * levels)
    steps = units // STEP
    return pl.pallas_call(
        functools.partial(synth_kernel, group, rows, levels, lats),
        grid=(steps,),
        in_specs=[
            pl.BlockSpec(memory_space=pltpu.SMEM),
            pl.BlockSpec((rows, 1), lambda i: (0, 0)),
            pl.BlockSpec((STEP, 2, 2, rows, part), lambda i: (i, 0, 0, 0, 0)),
            pl.BlockSpec((STEP, 16, part), lambda i: (i, 0, 0)),
            pl.BlockSpec((STEP // group, part, group * 2 * levels), lambda i: (i, 0, 0)),
            pl.BlockSpec((rows, 2 * lats, 2 * STEP), lambda i: (0, 0, i)),
        ],
        out_specs=[
            pl.BlockSpec((lats * 4 * rows, LANES), lambda i: (0, 0)),
            pl.BlockSpec((STEP, 16, LANES), lambda i: (i, 0, 0)),
        ],
        out_shape=[
            jax.ShapeDtypeStruct((lats * 4 * rows, LANES), jnp.float32),
            jax.ShapeDtypeStruct((units, 16, LANES), jnp.float32),
        ],
        scratch_shapes=[
            pltpu.VMEM((2, rows * 2 * STEP, LANES), jnp.float32),
            pltpu.VMEM((rows, 2, 2 * lats, LANES), jnp.float32),
        ],
        compiler_params=pltpu.CompilerParams(vmem_limit_bytes=56 * 1024 * 1024),
        cost_estimate=pl.CostEstimate(
            flops=units * rows * 4 * part * levels * 3, bytes_accessed=units * rows * 1024,
            transcendentals=0),
    )(ids, low, x, xd, w, tables)


def gathered_matrices(matrices, part):
    units, _, levels, _ = matrices.shape
    group = 2 if units % 2 == 0 else 1
    count = lax.axis_size("lev")
    turned = matrices.transpose(0, 3, 1, 2).reshape(units // group, group, count, part, 2 * levels)
    turned = turned.transpose(2, 0, 3, 1, 4)
    turned = turned.reshape(count, units // group, part, group * 2 * levels)
    if count == 2:
        lev = lax.axis_index("lev")
        kept = jnp.where(lev == 0, turned[0], turned[1])
        given = jnp.where(lev == 0, turned[1], turned[0])
        taken = lax.ppermute(given, "lev", [(0, 1), (1, 0)])
        both = jnp.stack([jnp.where(lev == 0, kept, taken), jnp.where(lev == 0, taken, kept)])
    else:
        both = lax.all_to_all(turned, "lev", split_axis=0, concat_axis=0, tiled=True)
    both = both.reshape(count * (units // group), part, group * 2 * levels)
    return lax.all_gather(both, "wave", axis=0, tiled=True)


def body(spec_main, spec_diag, pair_slots, correlation, balance, legendre, legendre_diag):
    part = spec_main.shape[1]
    slots = spec_main.shape[2]
    pairs = spec_main.shape[3] // 4
    here = correlation.shape[0]
    levels = correlation.shape[-1]
    lats = legendre.shape[1]
    shared = here % 2 == 0
    half = here // 2 if shared else here
    owners = pairs // here
    rows = -(-slots // 16) * 16
    fld = lax.axis_index("fld")

    own = correlation[:, :, 0]
    combined = jnp.einsum(
        "bskl,bslm->bskm", balance, own, preferred_element_type=jnp.float32
    ).astype(jnp.bfloat16)
    coupling = combined
    if shared:
        moved = lax.ppermute(combined[half:], "fld", [(0, 1)])
        coupling = jnp.where(fld == 0, combined[:half], moved)
    w_own = gathered_matrices(own, part)
    w_coupled = gathered_matrices(coupling, part)

    spec, diag = spec_main[0], spec_diag[0]
    other, other_diag = spec, diag
    if shared:
        other, other_diag = lax.ppermute((spec, diag), "fld", [(0, 1)])

    def halves(value, width):
        return value.reshape(value.shape[:-1] + (owners, 2, half * width))

    def chosen(mine, given, width):
        if not shared:
            return mine
        first = halves(mine, width)[..., 0, :]
        second = halves(given, width)[..., 1, :]
        picked = jnp.where(fld == 0, first, second)
        return picked.reshape(picked.shape[:-2] + (owners * half * width,))

    def entries(value):
        units = value.shape[-1] // 4
        turned = value.transpose(2, 1, 0).reshape(units, 2, 2, slots, part)
        return jnp.pad(turned, ((0, 0), (0, 0), (0, 0), (0, rows - slots), (0, 0)))

    pair_ids = jnp.arange(pairs, dtype=jnp.int32)
    half_ids = chosen(pair_ids, pair_ids, 1)

    def diag_entries(value, ids):
        onehot = (pair_slots[:, None] == ids[None, :]).astype(jnp.bfloat16)
        found = jnp.einsum(
            "krc,rb->bck", value.reshape(part, slots, 2), onehot,
            preferred_element_type=jnp.float32
        ).astype(jnp.bfloat16)
        return jnp.pad(found, ((0, 0), (0, 14), (0, 0)))

    low = jnp.pad(pair_slots, (0, rows - slots))[:, None]
    columns = jnp.arange(2 * pairs, dtype=jnp.int32)
    second = (columns % 2 == 1)[None, None, :]
    lower = (columns // 2)[None, None, :] >= pair_slots[:, None, None]
    nothing = jnp.zeros_like(legendre)
    tables = jnp.concatenate(
        [jnp.where(~second | lower, legendre, nothing),
         jnp.where(second & ~lower, legendre, nothing)], axis=1)
    tables = jnp.pad(tables, ((0, rows - slots), (0, 0), (0, 0)))
    half_tables = chosen(tables, tables, 2)

    own_orders = jnp.stack([pair_slots, NWAVE - 1 - pair_slots], axis=1)
    fourier_table = order_table(own_orders, NLON).reshape(slots * 4, NLON)
    fourier_table = jnp.pad(fourier_table, ((0, 4 * (rows - slots)), (0, 0)))

    def on_grid(ids, x, xd, w, table):
        coeffs, sector = synthesize(ids, low, x, xd, w, table, levels)
        picked = (pair_slots[:, None] == ids[None, :])
        at_slot = jnp.einsum(
            "rb,bck->rck", picked.astype(jnp.float32), sector[:, :2, :levels],
            precision=lax.Precision.HIGH, preferred_element_type=jnp.float32)
        at_slot = jnp.pad(at_slot, ((0, rows - slots), (0, 0), (0, 0)))
        sect_p = jnp.pad(legendre_diag.astype(jnp.float32), ((0, rows - slots), (0, 0)))
        extra = sect_p.T[:, :, None, None] * at_slot[None]
        extra = jnp.stack([jnp.zeros_like(extra), extra], axis=2)
        coeffs = coeffs.reshape(lats, 4 * rows, LANES)[:, :, :levels]
        coeffs = coeffs + extra.reshape(lats, 4 * rows, levels)
        return jnp.einsum("jqk,ql->jkl", coeffs, fourier_table,
                          precision=lax.Precision.HIGH, preferred_element_type=jnp.float32)

    grid_own = on_grid(pair_ids, entries(spec), diag_entries(diag, pair_ids), w_own, tables)
    x_half = entries(chosen(spec, other, 4))
    diag_half = jnp.where(fld == 0, diag, other_diag)
    grid_coupled = on_grid(
        half_ids, x_half, diag_entries(diag_half, half_ids), w_coupled, half_tables)
    arrived = lax.ppermute(grid_coupled, "fld", [(0, 1)])
    if shared:
        arrived = arrived + grid_coupled
    total = grid_own + jnp.where(fld == 0, 0.0, arrived)
    banded = lax.psum_scatter(total, "lev", scatter_dimension=1, tiled=True)
    banded = lax.psum_scatter(banded, "wave", scatter_dimension=0, tiled=True)
    return banded.transpose(1, 0, 2)[None]


def solution(mesh):
    return jax.shard_map(
        body,
        mesh=mesh,
        in_specs=(
            P(("members", "fld"), "lev", "wave", None),
            P(("members", "fld"), "lev", "wave"),
            P("wave"),
            P(("wave", "lev"), None, "fld", None, None),
            P(("wave", "lev"), None, None, None),
            P("wave", None, None),
            P("wave", None),
        ),
        out_specs=P(("members", "fld"), "lev", "wave", None),
        check_vma=False,
    )
```

```python
import functools
import math

import jax
import jax.numpy as jnp
from jax import lax
from jax.experimental import pallas as pl
from jax.experimental.pallas import tpu as pltpu
from jax.sharding import PartitionSpec as P

NWAVE = 768
NLON = 128
STEP = 64
LANES = 128


def order_table(orders, length):
    columns = jnp.arange(length, dtype=jnp.int32)
    phases = orders[..., None] * columns % (2 * NWAVE)
    angles = phases.astype(jnp.float32) * (math.pi / NWAVE)
    weight = jnp.where(orders == 0, 1.0, 2.0).astype(jnp.float32)[..., None]
    return jnp.stack([weight * jnp.cos(angles), -weight * jnp.sin(angles)], axis=-2)


def turn_kernel(part, rows, blocks, count, half, fld_ref, x_ref, xd_ref, out_ref, wide, turned):
    pitch = rows + 8
    for block in range(blocks):
        for k in range(part):
            wide[k * pitch:k * pitch + rows] = (
                x_ref[k, :, block * LANES:(block + 1) * LANES].astype(jnp.float32))

        def slot(g, carry, block=block):
            found = [wide[pl.ds(g * 16 + i, part, stride=pitch), :].T for i in range(16)]
            for i in range(16):
                turned[pl.ds(block * LANES * pitch + g * 16 + i, LANES, stride=pitch), 0:part] = found[i]
            return carry

        lax.fori_loop(0, rows // 16, slot, 0)

    def unit(g, carry):
        for i in range(2):
            u = g * 2 + i
            source = u if half is None else (u // half * 2 + fld_ref[0]) * half + u % half
            for q in range(4):
                start = pl.multiple_of((source * 4 + q) * pitch, 8)
                out_ref[u, q * rows:(q + 1) * rows, :] = (
                    turned[pl.ds(start, rows), :].astype(jnp.bfloat16))
            out_ref[u, 4 * rows:, 0:part] = xd_ref[u]
        return carry

    lax.fori_loop(0, count // 2, unit, 0)


def turn(fld, value, xd, half):
    part, rows, columns = value.shape
    lanes = LANES if half is None else 4 * 4 * half
    count = lanes // 4 if half is None else lanes // 8
    pitch = rows + 8
    return pl.pallas_call(
        functools.partial(turn_kernel, part, rows, lanes // LANES, count, half),
        grid=(columns // lanes,),
        in_specs=[
            pl.BlockSpec(memory_space=pltpu.SMEM),
            pl.BlockSpec((part, rows, lanes), lambda i: (0, 0, i)),
            pl.BlockSpec((count, 16, part), lambda i: (i, 0, 0)),
        ],
        out_specs=pl.BlockSpec((count, 4 * rows + 16, LANES), lambda i: (i, 0, 0)),
        out_shape=jax.ShapeDtypeStruct(
            (columns // lanes * count, 4 * rows + 16, LANES), jnp.bfloat16),
        scratch_shapes=[
            pltpu.VMEM((part * pitch, LANES), jnp.float32),
            pltpu.VMEM((lanes * pitch, LANES), jnp.float32),
        ],
        compiler_params=pltpu.CompilerParams(vmem_limit_bytes=56 * 1024 * 1024),
        cost_estimate=pl.CostEstimate(
            flops=0, bytes_accessed=100 * 1024 * 1024, transcendentals=0),
    )(fld, value, xd)


def synth_kernel(group, rows, levels, part, lats, ids_ref, low_ref, x_ref, w_ref, p_ref,
                 out_ref, diag_ref, ysc, acc):
    step = pl.program_id(0)
    steps = pl.num_programs(0)
    pitch = 2 * STEP + 8
    orders = jnp.concatenate([low_ref[...], low_ref[...]], axis=0)
    gap = jnp.zeros((part, LANES - levels), jnp.bfloat16)

    def units(g, carry):
        for e in range(16):
            u = g * 16 + e
            w = w_ref[g * (16 // group) + e // group]
            base = e % group * 2 * levels
            both = jnp.concatenate(
                [w[:, base + levels:base + 2 * levels], gap, w[:, base:base + levels], gap], axis=1)
            y = jnp.dot(x_ref[u, :, 0:part], both, preferred_element_type=jnp.float32)
            b = ids_ref[step * STEP + u]
            y1 = jnp.where(orders <= b, y[2 * rows:4 * rows, LANES:], y[2 * rows:4 * rows, :LANES])
            diag_ref[u] = y[4 * rows:, :LANES]
            for c in range(2):
                ysc[c, pl.ds(2 * u, rows, stride=pitch), :] = y[c * rows:(c + 1) * rows, :LANES]
                ysc[c, pl.ds(2 * u + 1, rows, stride=pitch), :] = y1[c * rows:(c + 1) * rows]
        return carry

    lax.fori_loop(0, STEP // 16, units, 0)

    @pl.when(step == 0)
    def _():
        acc[...] = jnp.zeros_like(acc)

    def slots(g, carry):
        sums = []
        for i in range(8):
            start = pl.multiple_of((g * 8 + i) * pitch, 8)
            y = jnp.concatenate(
                [ysc[c, pl.ds(start, 2 * STEP), :].astype(jnp.bfloat16) for c in range(2)], axis=1)
            sums.append(jnp.dot(p_ref[g * 8 + i], y, preferred_element_type=jnp.float32))
        for i in range(8):
            acc[g * 8 + i] += sums[i]
        return carry

    lax.fori_loop(0, rows // 8, slots, 0)

    @pl.when(step == steps - 1)
    def _():
        def spread(g, carry):
            for e in range(4):
                r = g * 4 + e
                for c in range(2):
                    for i in range(2):
                        out_ref[pl.ds(r * 4 + i * 2 + c, lats, stride=4 * rows), :] = (
                            acc[r, i * lats:(i + 1) * lats, c * LANES:(c + 1) * LANES])
            return carry

        lax.fori_loop(0, rows // 4, spread, 0)


def synthesize(ids, low, x, w, tables, levels):
    units, depth, _ = x.shape
    rows = tables.shape[0]
    part = w.shape[1]
    lats = tables.shape[1] // 2
    group = w.shape[-1] // (2 * levels)
    steps = units // STEP
    return pl.pallas_call(
        functools.partial(synth_kernel, group, rows, levels, part, lats),
        grid=(steps,),
        in_specs=[
            pl.BlockSpec(memory_space=pltpu.SMEM),
            pl.BlockSpec((rows, 1), lambda i: (0, 0)),
            pl.BlockSpec((STEP, depth, LANES), lambda i: (i, 0, 0)),
            pl.BlockSpec((STEP // group, part, group * 2 * levels), lambda i: (i, 0, 0)),
            pl.BlockSpec((rows, 2 * lats, 2 * STEP), lambda i: (0, 0, i)),
        ],
        out_specs=[
            pl.BlockSpec((lats * 4 * rows, LANES), lambda i: (0, 0)),
            pl.BlockSpec((STEP, 16, LANES), lambda i: (i, 0, 0)),
        ],
        out_shape=[
            jax.ShapeDtypeStruct((lats * 4 * rows, LANES), jnp.float32),
            jax.ShapeDtypeStruct((units, 16, LANES), jnp.float32),
        ],
        scratch_shapes=[
            pltpu.VMEM((2, rows * (2 * STEP + 8), LANES), jnp.float32),
            pltpu.VMEM((rows, 2 * lats, 2 * LANES), jnp.float32),
        ],
        compiler_params=pltpu.CompilerParams(vmem_limit_bytes=60 * 1024 * 1024),
        cost_estimate=pl.CostEstimate(
            flops=units * rows * 4 * part * levels * 3, bytes_accessed=units * rows * 2048,
            transcendentals=0),
    )(ids, low, x, w, tables)


def gathered_matrices(matrices, part):
    units, _, levels, _ = matrices.shape
    group = 2 if units % 2 == 0 else 1
    count = lax.axis_size("lev")
    turned = matrices.transpose(0, 3, 1, 2).reshape(units // group, group, count, part, 2 * levels)
    turned = turned.transpose(2, 0, 3, 1, 4)
    turned = turned.reshape(count, units // group, part, group * 2 * levels)
    if count == 2:
        lev = lax.axis_index("lev")
        kept = jnp.where(lev == 0, turned[0], turned[1])
        given = jnp.where(lev == 0, turned[1], turned[0])
        taken = lax.ppermute(given, "lev", [(0, 1), (1, 0)])
        both = jnp.stack([jnp.where(lev == 0, kept, taken), jnp.where(lev == 0, taken, kept)])
    else:
        both = lax.all_to_all(turned, "lev", split_axis=0, concat_axis=0, tiled=True)
    both = both.reshape(count * (units // group), part, group * 2 * levels)
    return lax.all_gather(both, "wave", axis=0, tiled=True)


def body(spec_main, spec_diag, pair_slots, correlation, balance, legendre, legendre_diag):
    part = spec_main.shape[1]
    slots = spec_main.shape[2]
    pairs = spec_main.shape[3] // 4
    here = correlation.shape[0]
    levels = correlation.shape[-1]
    lats = legendre.shape[1]
    shared = here % 16 == 0
    half = here // 2 if shared else here
    owners = pairs // here
    rows = -(-slots // 16) * 16
    fld = lax.axis_index("fld")

    own = correlation[:, :, 0]
    combined = jnp.einsum(
        "bskl,bslm->bskm", balance, own, preferred_element_type=jnp.float32
    ).astype(jnp.bfloat16)
    coupling = combined
    if shared:
        moved = lax.ppermute(combined[half:], "fld", [(0, 1)])
        coupling = jnp.where(fld == 0, combined[:half], moved)
    w_own = gathered_matrices(own, part)
    w_coupled = gathered_matrices(coupling, part)

    spec, diag = spec_main[0], spec_diag[0]
    other, other_diag = spec, diag
    if shared:
        other, other_diag = lax.ppermute((spec, diag), "fld", [(0, 1)])

    def halves(value, width):
        return value.reshape(value.shape[:-1] + (owners, 2, half * width))

    def chosen(mine, given, width):
        if not shared:
            return mine
        first = halves(mine, width)[..., 0, :]
        second = halves(given, width)[..., 1, :]
        picked = jnp.where(fld == 0, first, second)
        return picked.reshape(picked.shape[:-2] + (owners * half * width,))

    pair_ids = jnp.arange(pairs, dtype=jnp.int32)
    half_ids = chosen(pair_ids, pair_ids, 1)

    def diag_entries(value, ids):
        onehot = (pair_slots[:, None] == ids[None, :]).astype(jnp.bfloat16)
        found = jnp.einsum(
            "krc,rb->bck", value.reshape(part, slots, 2), onehot,
            preferred_element_type=jnp.float32
        ).astype(jnp.bfloat16)
        return jnp.pad(found, ((0, 0), (0, 14), (0, 0)))

    low = jnp.pad(pair_slots, (0, rows - slots))[:, None]
    columns = jnp.arange(2 * pairs, dtype=jnp.int32)
    second = (columns % 2 == 1)[None, None, :]
    lower = (columns // 2)[None, None, :] >= pair_slots[:, None, None]
    nothing = jnp.zeros_like(legendre)
    tables = jnp.concatenate(
        [jnp.where(~second | lower, legendre, nothing),
         jnp.where(second & ~lower, legendre, nothing)], axis=1)
    tables = jnp.pad(tables, ((0, rows - slots), (0, 0), (0, 0)))
    half_tables = chosen(tables, tables, 2)

    own_orders = jnp.stack([pair_slots, NWAVE - 1 - pair_slots], axis=1)
    fourier_table = order_table(own_orders, NLON).reshape(slots * 4, NLON)
    fourier_table = jnp.pad(fourier_table, ((0, 4 * (rows - slots)), (0, 0)))

    def on_grid(ids, x, w, table):
        coeffs, sector = synthesize(ids, low, x, w, table, levels)
        picked = (pair_slots[:, None] == ids[None, :])
        at_slot = jnp.einsum(
            "rb,bck->rck", picked.astype(jnp.float32), sector[:, :2, :levels],
            precision=lax.Precision.HIGH, preferred_element_type=jnp.float32)
        at_slot = jnp.pad(at_slot, ((0, rows - slots), (0, 0), (0, 0)))
        sect_p = jnp.pad(legendre_diag.astype(jnp.float32), ((0, rows - slots), (0, 0)))
        extra = sect_p.T[:, :, None, None] * at_slot[None]
        extra = jnp.stack([jnp.zeros_like(extra), extra], axis=2)
        coeffs = coeffs.reshape(lats, 4 * rows, LANES)[:, :, :levels]
        coeffs = coeffs + extra.reshape(lats, 4 * rows, levels)
        return jnp.einsum("jqk,ql->jkl", coeffs, fourier_table,
                          precision=lax.Precision.HIGH, preferred_element_type=jnp.float32)

    place = fld.astype(jnp.int32).reshape(1)
    padded = jnp.pad(spec, ((0, 0), (0, rows - slots), (0, 0)))
    x_own = turn(place, padded, diag_entries(diag, pair_ids), None)
    x_half = x_own
    if shared:
        source = jnp.where(fld == 0, spec, other)
        diag_half = jnp.where(fld == 0, diag, other_diag)
        source = jnp.pad(source, ((0, 0), (0, rows - slots), (0, 0)))
        x_half = turn(place, source, diag_entries(diag_half, half_ids), half)
    grid_own = on_grid(pair_ids, x_own, w_own, tables)
    grid_coupled = on_grid(half_ids, x_half, w_coupled, half_tables)
    arrived = lax.ppermute(grid_coupled, "fld", [(0, 1)])
    if shared:
        arrived = arrived + grid_coupled
    total = grid_own + jnp.where(fld == 0, 0.0, arrived)
    wave_count, lev_count = lax.axis_size("wave"), lax.axis_size("lev")
    total = total.reshape(wave_count, lats // wave_count, lev_count, part, NLON)
    total = total.transpose(0, 2, 3, 1, 4).reshape(owners, part, lats // wave_count, NLON)
    return lax.psum_scatter(total, ("wave", "lev"), scatter_dimension=0, tiled=True)


def solution(mesh):
    return jax.shard_map(
        body,
        mesh=mesh,
        in_specs=(
            P(("members", "fld"), "lev", "wave", None),
            P(("members", "fld"), "lev", "wave"),
            P("wave"),
            P(("wave", "lev"), None, "fld", None, None),
            P(("wave", "lev"), None, None, None),
            P("wave", None, None),
            P("wave", None),
        ),
        out_specs=P(("members", "fld"), "lev", "wave", None),
        check_vma=False,
    )
```

```python
import functools
import math

import jax
import jax.numpy as jnp
from jax import lax
from jax.experimental import pallas as pl
from jax.experimental.pallas import tpu as pltpu
from jax.sharding import PartitionSpec as P

NWAVE = 768
NLON = 128
STEP = 64
LANES = 128


def order_table(orders, length):
    columns = jnp.arange(length, dtype=jnp.int32)
    phases = orders[..., None] * columns % (2 * NWAVE)
    angles = phases.astype(jnp.float32) * (math.pi / NWAVE)
    weight = jnp.where(orders == 0, 1.0, 2.0).astype(jnp.float32)[..., None]
    return jnp.stack([weight * jnp.cos(angles), -weight * jnp.sin(angles)], axis=-2)


def turn_kernel(part, rows, blocks, count, half, fld_ref, x_ref, xd_ref, out_ref, wide, turned):
    pitch = rows + 8
    for block in range(blocks):
        for k in range(part):
            wide[k * pitch:k * pitch + rows] = (
                x_ref[k, :, block * LANES:(block + 1) * LANES].astype(jnp.float32))

        def slot(g, carry, block=block):
            found = [wide[pl.ds(g * 16 + i, part, stride=pitch), :].T for i in range(16)]
            for i in range(16):
                turned[pl.ds(block * LANES * pitch + g * 16 + i, LANES, stride=pitch), 0:part] = found[i]
            return carry

        lax.fori_loop(0, rows // 16, slot, 0)

    def unit(g, carry):
        for i in range(2):
            u = g * 2 + i
            source = u if half is None else (u // half * 2 + fld_ref[0]) * half + u % half
            for q in range(4):
                start = pl.multiple_of((source * 4 + q) * pitch, 8)
                out_ref[u, q * rows:(q + 1) * rows, :] = (
                    turned[pl.ds(start, rows), :].astype(jnp.bfloat16))
            out_ref[u, 4 * rows:, 0:part] = xd_ref[u]
        return carry

    lax.fori_loop(0, count // 2, unit, 0)


def turn(fld, value, xd, half):
    part, rows, columns = value.shape
    lanes = LANES if half is None else 4 * 4 * half
    count = lanes // 4 if half is None else lanes // 8
    pitch = rows + 8
    return pl.pallas_call(
        functools.partial(turn_kernel, part, rows, lanes // LANES, count, half),
        grid=(columns // lanes,),
        in_specs=[
            pl.BlockSpec(memory_space=pltpu.SMEM),
            pl.BlockSpec((part, rows, lanes), lambda i: (0, 0, i)),
            pl.BlockSpec((count, 16, part), lambda i: (i, 0, 0)),
        ],
        out_specs=pl.BlockSpec((count, 4 * rows + 16, LANES), lambda i: (i, 0, 0)),
        out_shape=jax.ShapeDtypeStruct(
            (columns // lanes * count, 4 * rows + 16, LANES), jnp.bfloat16),
        scratch_shapes=[
            pltpu.VMEM((part * pitch, LANES), jnp.float32),
            pltpu.VMEM((lanes * pitch, LANES), jnp.float32),
        ],
        compiler_params=pltpu.CompilerParams(vmem_limit_bytes=56 * 1024 * 1024),
        cost_estimate=pl.CostEstimate(
            flops=0, bytes_accessed=100 * 1024 * 1024, transcendentals=0),
    )(fld, value, xd)


def synth_kernel(group, rows, levels, part, lats, ids_ref, low_ref, x_ref, w_ref, p_ref,
                 out_ref, diag_ref, ysc, acc):
    step = pl.program_id(0)
    steps = pl.num_programs(0)
    pitch = 2 * STEP + 8
    orders = jnp.concatenate([low_ref[...], low_ref[...]], axis=0)
    gap = jnp.zeros((part, LANES - levels), jnp.bfloat16)

    def units(g, carry):
        for e in range(16):
            u = g * 16 + e
            w = w_ref[g * (16 // group) + e // group]
            base = e % group * 2 * levels
            both = jnp.concatenate(
                [w[:, base + levels:base + 2 * levels], gap, w[:, base:base + levels], gap], axis=1)
            y = jnp.dot(x_ref[u, :, 0:part], both, preferred_element_type=jnp.float32)
            b = ids_ref[step * STEP + u]
            y1 = jnp.where(orders <= b, y[2 * rows:4 * rows, LANES:], y[2 * rows:4 * rows, :LANES])
            diag_ref[u] = y[4 * rows:, :LANES]
            for c in range(2):
                ysc[c, pl.ds(2 * u, rows, stride=pitch), :] = y[c * rows:(c + 1) * rows, :LANES]
                ysc[c, pl.ds(2 * u + 1, rows, stride=pitch), :] = y1[c * rows:(c + 1) * rows]
        return carry

    lax.fori_loop(0, STEP // 16, units, 0)

    @pl.when(step == 0)
    def _():
        acc[...] = jnp.zeros_like(acc)

    def slots(g, carry):
        sums = []
        for i in range(8):
            start = pl.multiple_of((g * 8 + i) * pitch, 8)
            y = jnp.concatenate(
                [ysc[c, pl.ds(start, 2 * STEP), :].astype(jnp.bfloat16) for c in range(2)], axis=1)
            sums.append(jnp.dot(p_ref[g * 8 + i], y, preferred_element_type=jnp.float32))
        for i in range(8):
            acc[g * 8 + i] += sums[i]
        return carry

    lax.fori_loop(0, rows // 8, slots, 0)

    @pl.when(step == steps - 1)
    def _():
        def spread(g, carry):
            for e in range(4):
                r = g * 4 + e
                for c in range(2):
                    for i in range(2):
                        out_ref[pl.ds(r * 4 + i * 2 + c, lats, stride=4 * rows), :] = (
                            acc[r, i * lats:(i + 1) * lats, c * LANES:(c + 1) * LANES])
            return carry

        lax.fori_loop(0, rows // 4, spread, 0)


def synthesize(ids, low, x, w, tables, levels):
    units, depth, _ = x.shape
    rows = tables.shape[0]
    part = w.shape[1]
    lats = tables.shape[1] // 2
    group = w.shape[-1] // (2 * levels)
    steps = units // STEP
    return pl.pallas_call(
        functools.partial(synth_kernel, group, rows, levels, part, lats),
        grid=(steps,),
        in_specs=[
            pl.BlockSpec(memory_space=pltpu.SMEM),
            pl.BlockSpec((rows, 1), lambda i: (0, 0)),
            pl.BlockSpec((STEP, depth, LANES), lambda i: (i, 0, 0)),
            pl.BlockSpec((STEP // group, part, group * 2 * levels), lambda i: (i, 0, 0)),
            pl.BlockSpec((rows, 2 * lats, 2 * STEP), lambda i: (0, 0, i)),
        ],
        out_specs=[
            pl.BlockSpec((lats * 4 * rows, LANES), lambda i: (0, 0)),
            pl.BlockSpec((STEP, 16, LANES), lambda i: (i, 0, 0)),
        ],
        out_shape=[
            jax.ShapeDtypeStruct((lats * 4 * rows, LANES), jnp.float32),
            jax.ShapeDtypeStruct((units, 16, LANES), jnp.float32),
        ],
        scratch_shapes=[
            pltpu.VMEM((2, rows * (2 * STEP + 8), LANES), jnp.float32),
            pltpu.VMEM((rows, 2 * lats, 2 * LANES), jnp.float32),
        ],
        compiler_params=pltpu.CompilerParams(vmem_limit_bytes=60 * 1024 * 1024),
        cost_estimate=pl.CostEstimate(
            flops=units * rows * 4 * part * levels * 3, bytes_accessed=units * rows * 2048,
            transcendentals=0),
    )(ids, low, x, w, tables)


def gathered_matrices(matrices, part):
    units, _, levels, _ = matrices.shape
    group = 2 if units % 2 == 0 else 1
    count = lax.axis_size("lev")
    turned = matrices.transpose(0, 3, 1, 2).reshape(units // group, group, count, part, 2 * levels)
    turned = turned.transpose(2, 0, 3, 1, 4)
    turned = turned.reshape(count, units // group, part, group * 2 * levels)
    if count == 2:
        lev = lax.axis_index("lev")
        kept = jnp.where(lev == 0, turned[0], turned[1])
        given = jnp.where(lev == 0, turned[1], turned[0])
        taken = lax.ppermute(given, "lev", [(0, 1), (1, 0)])
        both = jnp.stack([jnp.where(lev == 0, kept, taken), jnp.where(lev == 0, taken, kept)])
    else:
        both = lax.all_to_all(turned, "lev", split_axis=0, concat_axis=0, tiled=True)
    both = both.reshape(count * (units // group), part, group * 2 * levels)
    return lax.all_gather(both, "wave", axis=0, tiled=True)


def body(spec_main, spec_diag, pair_slots, correlation, balance, legendre, legendre_diag):
    part = spec_main.shape[1]
    slots = spec_main.shape[2]
    pairs = spec_main.shape[3] // 4
    here = correlation.shape[0]
    levels = correlation.shape[-1]
    lats = legendre.shape[1]
    shared = here % 16 == 0
    half = here // 2 if shared else here
    owners = pairs // here
    rows = -(-slots // 16) * 16
    fld = lax.axis_index("fld")

    own = correlation[:, :, 0]
    combined = jnp.einsum(
        "bskl,bslm->bskm", balance, own, preferred_element_type=jnp.float32
    ).astype(jnp.bfloat16)
    coupling = combined
    if shared:
        moved = lax.ppermute(combined[half:], "fld", [(0, 1)])
        coupling = jnp.where(fld == 0, combined[:half], moved)
    w_own = gathered_matrices(own, part)
    w_coupled = gathered_matrices(coupling, part)

    spec, diag = spec_main[0], spec_diag[0]
    other, other_diag = spec, diag
    if shared:
        other, other_diag = lax.ppermute((spec, diag), "fld", [(0, 1)])

    def halves(value, width):
        return value.reshape(value.shape[:-1] + (owners, 2, half * width))

    def chosen(mine, given, width):
        if not shared:
            return mine
        first = halves(mine, width)[..., 0, :]
        second = halves(given, width)[..., 1, :]
        picked = jnp.where(fld == 0, first, second)
        return picked.reshape(picked.shape[:-2] + (owners * half * width,))

    pair_ids = jnp.arange(pairs, dtype=jnp.int32)
    half_ids = chosen(pair_ids, pair_ids, 1)

    def diag_entries(value, ids):
        onehot = (pair_slots[:, None] == ids[None, :]).astype(jnp.bfloat16)
        found = jnp.einsum(
            "krc,rb->bck", value.reshape(part, slots, 2), onehot,
            preferred_element_type=jnp.float32
        ).astype(jnp.bfloat16)
        return jnp.pad(found, ((0, 0), (0, 14), (0, 0)))

    low = jnp.pad(pair_slots, (0, rows - slots))[:, None]
    def masked(values, ids):
        second = (jnp.arange(values.shape[-1], dtype=jnp.int32) % 2 == 1)[None, None, :]
        lower = jnp.repeat(ids, 2)[None, None, :] >= pair_slots[:, None, None]
        nothing = jnp.zeros_like(values)
        both = jnp.concatenate(
            [jnp.where(~second | lower, values, nothing),
             jnp.where(second & ~lower, values, nothing)], axis=1)
        return jnp.pad(both, ((0, rows - slots), (0, 0), (0, 0)))

    tables = masked(legendre, pair_ids)
    half_tables = masked(chosen(legendre, legendre, 2), half_ids) if shared else tables

    own_orders = jnp.stack([pair_slots, NWAVE - 1 - pair_slots], axis=1)
    fourier_table = order_table(own_orders, NLON).reshape(slots * 4, NLON)
    fourier_table = jnp.pad(fourier_table, ((0, 4 * (rows - slots)), (0, 0)))

    def on_grid(ids, x, w, table):
        coeffs, sector = synthesize(ids, low, x, w, table, levels)
        picked = (pair_slots[:, None] == ids[None, :])
        at_slot = jnp.einsum(
            "rb,bck->rck", picked.astype(jnp.float32), sector[:, :2, :levels],
            precision=lax.Precision.HIGH, preferred_element_type=jnp.float32)
        at_slot = jnp.pad(at_slot, ((0, rows - slots), (0, 0), (0, 0)))
        sect_p = jnp.pad(legendre_diag.astype(jnp.float32), ((0, rows - slots), (0, 0)))
        extra = sect_p.T[:, :, None, None] * at_slot[None]
        extra = jnp.stack([jnp.zeros_like(extra), extra], axis=2)
        coeffs = coeffs.reshape(lats, 4 * rows, LANES)[:, :, :levels]
        coeffs = coeffs + extra.reshape(lats, 4 * rows, levels)
        return jnp.einsum("jqk,ql->jkl", coeffs, fourier_table,
                          precision=lax.Precision.HIGH, preferred_element_type=jnp.float32)

    place = fld.astype(jnp.int32).reshape(1)
    padded = jnp.pad(spec, ((0, 0), (0, rows - slots), (0, 0)))
    x_own = turn(place, padded, diag_entries(diag, pair_ids), None)
    x_half = x_own
    if shared:
        source = jnp.where(fld == 0, spec, other)
        diag_half = jnp.where(fld == 0, diag, other_diag)
        source = jnp.pad(source, ((0, 0), (0, rows - slots), (0, 0)))
        x_half = turn(place, source, diag_entries(diag_half, half_ids), half)
        x_own, x_half = lax.optimization_barrier((x_own, x_half))
    grid_own = on_grid(pair_ids, x_own, w_own, tables)
    grid_coupled = on_grid(half_ids, x_half, w_coupled, half_tables)
    arrived = lax.ppermute(grid_coupled, "fld", [(0, 1)])
    if shared:
        arrived = arrived + grid_coupled
    total = grid_own + jnp.where(fld == 0, 0.0, arrived)
    if lax.axis_size("lev") == 2:
        lev = lax.axis_index("lev")
        kept = jnp.where(lev == 0, total[:, :part], total[:, part:])
        given = jnp.where(lev == 0, total[:, part:], total[:, :part])
        banded = kept + lax.ppermute(given, "lev", [(0, 1), (1, 0)])
    else:
        banded = lax.psum_scatter(total, "lev", scatter_dimension=1, tiled=True)
    banded = lax.psum_scatter(banded, "wave", scatter_dimension=0, tiled=True)
    return banded.transpose(1, 0, 2)[None]


def solution(mesh):
    return jax.shard_map(
        body,
        mesh=mesh,
        in_specs=(
            P(("members", "fld"), "lev", "wave", None),
            P(("members", "fld"), "lev", "wave"),
            P("wave"),
            P(("wave", "lev"), None, "fld", None, None),
            P(("wave", "lev"), None, None, None),
            P("wave", None, None),
            P("wave", None),
        ),
        out_specs=P(("members", "fld"), "lev", "wave", None),
        check_vma=False,
    )
```
